512 devices in a mesh: leaf: 128 (over y, z, core), rhs: 4 (over x).
Axes of the slice: x: 4, y: 4, z: 16, core: 2. Of those that a mesh axis runs over, the one named last changes fastest.
Arguments:
- leaf_rhs: bfloat16 [262144, 512], P('leaf', 'rhs'), may hold values from -6 to 6
- leaf_inverse: bfloat16 [2048, 128, 128], P('leaf'), as said below
- panels: bfloat16 [2048, 4, 128, 128], P('leaf'), may hold values from -0.02734375 to 0.02734375
- ancestors: int32 [2048, 4], P('leaf'), may hold values from 0 to 7, as said below
- pattern: int32 [2048, 4], P('leaf'), may hold values 0 or 1
- top_rhs: bfloat16 [1024, 512], P(None, 'rhs'), may hold values from -6 to 6
- top_inverse: bfloat16 [4, 256, 256], P('rhs'), as said below
Outputs:
- leaf_solution: float32 [262144, 512], P('leaf', 'rhs')
- top_solution: bfloat16 [1024, 512], P(None, 'rhs')
The draws below stay inside these ranges and needn't reach their ends.
Inputs may be any that keep to these rules, and one draw needn't show every extreme that they name: `ancestors`: each leaf's 4 entries are distinct row blocks, consecutive modulo 8. `leaf_inverse`: lower triangular with a diagonal of positive entries. `top_inverse`: lower triangular with a diagonal of positive entries.
All inputs are finite; a program needn't handle non-finite values. No bound on the sum of `pattern` on one device may be relied on, other than what follows from the above.
Results may differ from the reference program's by a relative error of at most 0.014.
Values may be sent and summed in bfloat16 or wider, within the bound.
A program may use at most 64 MiB of HBM per device.

```python
import math
import jax
import jax.numpy as jnp
from jax import lax

W = 128
WT = 256
BLK = 128
TOPS = 4
K = 4
NRHS = 512
LEAVES = 2048
R = 1024
RB = 8


def lower_factor(key, number, order, spread):
    diagonal = jax.random.uniform(jax.random.fold_in(key, 1), (number, order), jnp.float32, 0.6, 1.5)
    entries = jax.random.normal(jax.random.fold_in(key, 2), (number, order, order), jnp.float32) * (spread / math.sqrt(order))
    row_ids = jnp.arange(order)[:, None]
    col_ids = jnp.arange(order)[None, :]
    strict = (row_ids > col_ids).astype(jnp.float32)
    identity = (row_ids == col_ids).astype(jnp.float32)
    return entries * strict + diagonal[:, :, None] * identity


def draw_leaf_inverse(key, part):
    key = jax.random.fold_in(key, 11)
    return lower_factor(key, LEAVES, W, 0.6).astype(jnp.bfloat16)


def draw_top_inverse(key, part):
    key = jax.random.fold_in(key, 17)
    return lower_factor(key, TOPS, WT, 0.6).astype(jnp.bfloat16)


def draw_ancestors(key, part):
    key = jax.random.fold_in(key, 23)
    first_block = jax.random.randint(key, (LEAVES, 1), 0, RB)
    return ((first_block + jnp.arange(K)[None, :]) % RB).astype(jnp.int32)


def place_ends(values, own_key, least, largest):
    place = [jax.random.randint(jax.random.fold_in(own_key, axis), (), 0, length) for axis, length in enumerate(values.shape)]
    widest = values.shape.index(max(values.shape))
    neighbour = place[:widest] + [(place[widest] + 1) % values.shape[widest]] + place[widest + 1:]
    return values.at[tuple(place)].set(least).at[tuple(neighbour)].set(largest)


def level_of(key, extent, cuts, smallest, high):
    gain = 1.0
    for axis_at, parts in cuts:
        draws = jax.random.uniform(jax.random.fold_in(jax.random.fold_in(key, 6), axis_at), (parts,), jnp.float32, smallest / len(cuts), high / len(cuts))
        gain = gain * jnp.repeat(jnp.exp(draws), extent[axis_at] // parts).reshape((-1,) + (1,) * (len(extent) - 1 - axis_at))
    return gain


def normal_values(key, shape, scale, bound, split=(), held_as=jnp.bfloat16):
    values = scale * jax.random.normal(key, shape, jnp.float32)
    if split:
        values = values * level_of(key, shape, split, -0.22, 0.18)
    return jnp.clip(values, -bound, bound).astype(held_as)


def setup_inputs(seed: int = 0) -> dict:
    keys = jax.random.split(jax.random.key(seed), 8)
    leaf_rhs = normal_values(keys[0], (LEAVES * W, NRHS), 1.0, 6.0, ((0, 128), (1, 4)))
    leaf_inverse = draw_leaf_inverse(jax.random.fold_in(keys[7], 71), 0)
    panels = normal_values(keys[2], (LEAVES, K, BLK, W), (0.7 * (W * LEAVES * K // RB) ** -0.5), 0.02734375, ((0, 128),))
    ancestors = draw_ancestors(jax.random.fold_in(keys[7], 71), 0)
    pattern = place_ends((jax.random.randint(keys[4], (LEAVES, K), 0, 4) < 3).astype(jnp.int32), jax.random.fold_in(keys[4], 1), 0, 1)
    top_rhs = normal_values(keys[5], (R, NRHS), 1.0, 6.0, ((1, 4),))
    top_inverse = draw_top_inverse(jax.random.fold_in(keys[7], 71), 0)
    return dict(leaf_rhs=leaf_rhs, leaf_inverse=leaf_inverse, panels=panels, ancestors=ancestors, pattern=pattern, top_rhs=top_rhs, top_inverse=top_inverse)


def leaf_forward(inv_group, rhs_group, panel_group, select_group):
    solved = jnp.einsum('lij,ljc->lic', inv_group.astype(jnp.float32), rhs_group.astype(jnp.float32)).astype(jnp.bfloat16)
    terms = jnp.einsum('lkpj,ljc->lkpc', panel_group.astype(jnp.float32), solved.astype(jnp.float32))
    update = jnp.einsum('lkb,lkpc->bpc', select_group, terms)
    return solved, update


def reference(leaf_rhs, leaf_inverse, panels, ancestors, pattern, top_rhs, top_inverse):
    select = (ancestors[:, :, None] == jnp.arange(RB, dtype=jnp.int32)[None, None, :]).astype(jnp.float32)
    select = select * pattern[:, :, None].astype(jnp.float32)
    groups = LEAVES // 16
    rhs_all = leaf_rhs.reshape(groups, 16, W, NRHS)
    inv_all = leaf_inverse.reshape(groups, 16, W, W)
    panel_all = panels.reshape(groups, 16, K, BLK, W)
    select_all = select.reshape(groups, 16, K, RB)

    def forward(update_sum, pieces):
        solved, update = leaf_forward(pieces[0], pieces[1], pieces[2], pieces[3])
        return update_sum + update, solved

    update_sum, solved_all = lax.scan(forward, jnp.zeros((RB, BLK, NRHS), jnp.float32), (inv_all, rhs_all, panel_all, select_all))
    reduced = (top_rhs.astype(jnp.float32) - update_sum.reshape(R, NRHS)).astype(jnp.bfloat16)
    middle = jnp.einsum('tij,tjc->tic', top_inverse.astype(jnp.float32), reduced.reshape(TOPS, WT, NRHS).astype(jnp.float32)).astype(jnp.bfloat16)
    top_solution = jnp.einsum('tji,tjc->tic', top_inverse.astype(jnp.float32), middle.astype(jnp.float32)).astype(jnp.bfloat16).reshape(R, NRHS)
    known = top_solution.reshape(RB, BLK, NRHS).astype(jnp.float32)

    def backward(state_value, pieces):
        gathered = jnp.einsum('lkb,bpc->lkpc', pieces[2], known)
        back_sum = jnp.einsum('lkpj,lkpc->ljc', pieces[1].astype(jnp.float32), gathered)
        remainder = (pieces[3].astype(jnp.float32) - back_sum).astype(jnp.bfloat16)
        result = jnp.einsum('lji,ljc->lic', pieces[0].astype(jnp.float32), remainder.astype(jnp.float32))
        return state_value, result

    _, leaf_solution = lax.scan(backward, jnp.zeros((), jnp.float32), (inv_all, panel_all, select_all, solved_all))
    return leaf_solution.reshape(LEAVES * W, NRHS), top_solution
```

```python
import functools
import jax
import jax.numpy as jnp
from jax import lax
from jax.experimental import pallas as pl
from jax.experimental.pallas import tpu as pltpu
from jax.sharding import PartitionSpec as P

MESH = pl.DeviceIdType.MESH
BF = jnp.bfloat16
F32 = jnp.float32
NY, NZ = 4, 16
LV = 16
NB = 8


def place():
    leaf = lax.axis_index("leaf")
    return leaf // (2 * NZ), (leaf // 2) % NZ, leaf % 2, lax.axis_index("rhs")


def device(y, z, c, x):
    return ((y * NZ + z) * 2 + c, x)


def send(src, dst, send_sem, recv_sem, to):
    pltpu.make_async_remote_copy(
        src_ref=src, dst_ref=dst, send_sem=send_sem, recv_sem=recv_sem, device_id=to, device_id_type=MESH
    ).start()


def take(like, sem):
    pltpu.make_async_copy(like, like, sem).wait()


def forward_kernel(
    rhs_h, inv_h, pan_h, anc, pat, trhs_h, tinv_h, s_out, x_out,
    rhs, inv, pan, solved, acc, own, half_tx, half_rx, tx1, rx1, tx2, rx2, trhs, red, tops, xs,
    in_sem, out_sem, half_s, half_r, s1_s, s1_r, s2_s, s2_r, s3_s, s3_r, s4_s, s4_r, t_s, t_r,
):
    y, z, c, x = place()
    zr, za = z % 4, z // 4
    grp = y * 4 + zr
    bar = pltpu.get_barrier_semaphore()

    def greet(to):
        pl.semaphore_signal(bar, inc=1, device_id=to, device_id_type=MESH)

    greet(device(y, z, 1 - c, x))
    for dy in range(4):
        for d in (-2, -1, 0, 1):
            if (dy, d) != (0, 0):
                greet(device((y - dy) % 4, (z - d) % NZ, c, x))
    for k in (1, 2, 3):
        greet(device(y, (z + 4 * k) % NZ, c, x))
        greet(device(y, z, c, (x + k) % 4))

    loads = [
        pltpu.make_async_copy(rhs_h, rhs, in_sem.at[0]),
        pltpu.make_async_copy(inv_h, inv, in_sem.at[1]),
        pltpu.make_async_copy(pan_h, pan.at[:, pl.ds(0, 4)], in_sem.at[2]),
        pltpu.make_async_copy(tinv_h.at[0], tops.at[x], in_sem.at[3]),
        pltpu.make_async_copy(
            trhs_h.at[pl.ds(pl.multiple_of((grp // 2) * 128 + c * 64 + (grp % 2) * 32, 32), 32)], trhs, in_sem.at[4]
        ),
    ]
    for load in loads:
        load.start()
    pan[:, 4] = jnp.zeros((LV, 128, 128), BF)
    loads[0].wait()
    loads[1].wait()

    def solve(l, _):
        rows = pl.ds(pl.multiple_of(l * 128, 128), 128)
        solved[rows] = jnp.dot(inv[l], rhs[rows], preferred_element_type=F32).astype(BF)
        return 0

    lax.fori_loop(0, LV, solve, 0, unroll=4)
    s_copy = pltpu.make_async_copy(solved, s_out, out_sem.at[0])
    s_copy.start()
    loads[2].wait()
    loads[3].wait()
    pl.semaphore_wait(bar, 22)
    for k in (1, 2, 3):
        send(tops.at[x], tops.at[x], t_s, t_r, device(y, z, c, (x + k) % 4))

    def spread(i):
        to_y = (y + 1 + i // 2) % 4
        dy = (1 + i // 2) % 4
        take(half_rx.at[i], half_r.at[i])
        tx1[i] = (own[i] + half_rx[i].astype(F32)).astype(BF)
        for h in range(2):
            r = 2 * (i % 2) + h
            d = (r - z + 2) % 4
            slot = dy * 4 + d
            piece = tx1.at[i, pl.ds(h * 32, 32)]
            mine = (dy == 0) & (d == 2)

            @pl.when(jnp.logical_not(mine))
            def _():
                send(piece, rx1.at[slot], s1_s, s1_r, device(to_y, (z + d - 2) % NZ, c, x))

            @pl.when(mine)
            def _():
                rx1[2] = piece[...]

    def block(i, _):
        b = 2 * ((y + 1 + i // 2) % 4) + i % 2
        parts = []
        for l in range(LV):
            kk = 4
            for k in range(4):
                kk = jnp.where((anc[l, k] == b) & (pat[l, k] != 0), k, kk)
            parts.append(pan[l, kk])
        acc[...] = jnp.dot(jnp.concatenate(parts, axis=1), solved[...], preferred_element_type=F32)
        half_tx[i] = acc[pl.ds(pl.multiple_of((1 - c) * 64, 64), 64)].astype(BF)
        send(half_tx.at[i], half_rx.at[i], half_s, half_r.at[i], device(y, z, 1 - c, x))
        own[i] = acc[pl.ds(pl.multiple_of(c * 64, 64), 64)]

        @pl.when(i > 0)
        def _():
            spread(i - 1)

        return 0

    lax.fori_loop(0, NB, block, 0)
    spread(NB - 1)

    take(rx1.at[pl.ds(0, 15)], s1_r)
    total = rx1[0].astype(F32)
    for slot in range(1, 16):
        total = total + rx1[slot].astype(F32)
    tx2[...] = total.astype(BF)
    for k in (2, 1, 3):
        send(tx2, rx2.at[za], s2_s, s2_r, device(y, (z + 4 * k) % NZ, c, x))
    rx2[za] = tx2[...]
    loads[4].wait()
    take(rx2.at[pl.ds(0, 3)], s2_r)
    total = rx2[0].astype(F32)
    for k in range(1, 4):
        total = total + rx2[k].astype(F32)
    red[c, grp] = (trhs[...].astype(F32) - total).astype(BF)
    piece = red.at[c, grp]
    for dy in (2, 1, 3, 0):
        for d in (-2, 1, -1, 0):
            if (dy, d) != (0, 0):
                send(piece, piece, s3_s, s3_r.at[dy], device((y + dy) % 4, (z + d) % NZ, c, x))
    for dy in (0, 1, 3, 2):
        from_y = (y - dy) % 4
        quarter = red.at[c, pl.ds(pl.multiple_of(from_y * 4, 4), 4)]
        take(red.at[c, pl.ds(0, 3 if dy == 0 else 4)], s3_r.at[dy])
        send(quarter, quarter, s4_s, s4_r.at[dy], device(y, z, 1 - c, x))
    take(tops.at[pl.ds(0, 3)], t_r)
    for dy in (0, 1, 3, 2):
        t = (y - dy) % 4
        take(red.at[c, pl.ds(0, 4)], s4_r.at[dy])
        parts = []
        for j in range(2):
            for core in range(2):
                for h in range(2):
                    parts.append(red[core, t * 4 + 2 * j + h])
        reduced = jnp.concatenate(parts, axis=0)
        middle = jnp.dot(tops[t], reduced, preferred_element_type=F32).astype(BF)
        xs[t] = lax.dot_general(tops[t], middle, (((0,), (0,)), ((), ())), preferred_element_type=F32).astype(BF)
    x_copy = pltpu.make_async_copy(xs, x_out, out_sem.at[1])
    x_copy.start()
    take(half_tx, half_s)
    take(rx1.at[pl.ds(0, 15)], s1_s)
    take(rx2.at[pl.ds(0, 3)], s2_s)
    take(rx1.at[pl.ds(0, 15)], s3_s)
    take(red.at[c], s4_s)
    take(tops.at[pl.ds(0, 3)], t_s)
    s_copy.wait()
    x_copy.wait()


def backward_kernel(inv, pan, solved, xs, anc, pat, out, x_out, known):
    known[pl.ds(0, NB)] = xs[...]
    known[NB] = jnp.zeros((128, 128), BF)
    x_out[...] = xs[...]
    for l in range(LV):
        parts = []
        for k in range(4):
            parts.append(known[jnp.where(pat[l, k] != 0, anc[l, k], NB)])
        back = lax.dot_general(
            pan[l].reshape(512, 128), jnp.concatenate(parts, axis=0), (((0,), (0,)), ((), ())), preferred_element_type=F32
        )
        rem = (solved[l].astype(F32) - back).astype(BF)
        out[l] = lax.dot_general(inv[l], rem, (((0,), (0,)), ((), ())), preferred_element_type=F32)


def shards(leaf_rhs, leaf_inverse, panels, ancestors, pattern, top_rhs, top_inverse):
    any_spec = pl.BlockSpec(memory_space=pl.ANY)
    smem = pl.BlockSpec(memory_space=pltpu.SMEM)
    vmem = pl.BlockSpec(memory_space=pltpu.VMEM)
    V, D = pltpu.VMEM, pltpu.SemaphoreType.DMA
    solved, xs = pl.pallas_call(
        forward_kernel,
        out_shape=(jax.ShapeDtypeStruct((2048, 128), BF), jax.ShapeDtypeStruct((4, 256, 128), BF)),
        in_specs=[any_spec, any_spec, any_spec, smem, smem, any_spec, any_spec],
        out_specs=(any_spec, any_spec),
        scratch_shapes=[
            V((2048, 128), BF), V((LV, 128, 128), BF), V((LV, 5, 128, 128), BF), V((2048, 128), BF),
            V((128, 128), F32), V((NB, 64, 128), F32), V((NB, 64, 128), BF), V((NB, 64, 128), BF),
            V((NB, 64, 128), BF), V((16, 32, 128), BF), V((32, 128), BF), V((4, 32, 128), BF),
            V((32, 128), BF), V((2, 16, 32, 128), BF), V((4, 256, 256), BF), V((4, 256, 128), BF),
            D((5,)), D((2,)), D, D((NB,)), D, D, D, D, D, D((4,)), D, D((4,)), D, D,
        ],
        compiler_params=pltpu.CompilerParams(collective_id=0, has_side_effects=True, vmem_limit_bytes=24 * 2**20),
        cost_estimate=pl.CostEstimate(flops=700_000_000, bytes_accessed=4_000_000, transcendentals=0),
        name="forward",
    )(leaf_rhs, leaf_inverse, panels, ancestors, pattern, top_rhs, top_inverse)
    leaf_solution, top_solution = pl.pallas_call(
        backward_kernel,
        out_shape=(jax.ShapeDtypeStruct((LV, 128, 128), F32), jax.ShapeDtypeStruct((NB, 128, 128), BF)),
        in_specs=[vmem, vmem, vmem, vmem, smem, smem],
        out_specs=(vmem, vmem),
        scratch_shapes=[V((NB + 1, 128, 128), BF)],
        compiler_params=pltpu.CompilerParams(vmem_limit_bytes=24 * 2**20),
        cost_estimate=pl.CostEstimate(flops=400_000_000, bytes_accessed=4_000_000, transcendentals=0),
        name="backward",
    )(leaf_inverse, panels, solved.reshape(LV, 128, 128), xs.reshape(NB, 128, 128), ancestors, pattern)
    return leaf_solution.reshape(LV * 128, 128), top_solution.reshape(NB * 128, 128)


def solution(mesh):
    placed = (
        P("leaf", "rhs"),
        P("leaf", None, None),
        P("leaf", None, None, None),
        P("leaf", None),
        P("leaf", None),
        P(None, "rhs"),
        P("rhs", None, None),
    )
    return jax.shard_map(
        shards, mesh=mesh, in_specs=placed, out_specs=(P("leaf", "rhs"), P(None, "rhs")), check_vma=False
    )
```

```python
import functools
import jax
import jax.numpy as jnp
from jax import lax
from jax.experimental import pallas as pl
from jax.experimental.pallas import tpu as pltpu
from jax.sharding import PartitionSpec as P

MESH = pl.DeviceIdType.MESH
BF = jnp.bfloat16
F32 = jnp.float32
NY, NZ = 4, 16
LV = 16
NB = 8
CHAIN = True
TSEND = True
ORDER = (2, 1, 3, 0)
PER = 2


def place():
    leaf = lax.axis_index("leaf")
    return leaf // (2 * NZ), (leaf // 2) % NZ, leaf % 2, lax.axis_index("rhs")


def device(y, z, c, x):
    return ((y * NZ + z) * 2 + c, x)


def send(src, dst, send_sem, recv_sem, to):
    pltpu.make_async_remote_copy(
        src_ref=src, dst_ref=dst, send_sem=send_sem, recv_sem=recv_sem, device_id=to, device_id_type=MESH
    ).start()


def take(like, sem):
    pltpu.make_async_copy(like, like, sem).wait()


def forward_kernel(
    rhs_h, inv_h, pan_h, anc_h, pat_h, trhs_h, tinv_h, solved_o, flip_o, invt_o, tops_o, topt_o, red_o,
    rhs, inv, pan, anc, pat, which, solved, flip, invt, tops, topt,
    half_tx, half_rx, tx1, rx1, tx2, rx2, trhs, mine_red,
    in_sem, out_sem, near, far, half_s, half_r, s1_s, s1_r, s2_s, s2_r, s3_s, s3_r, s4_s, s4_r, t_s, t_r,
):
    y, z, c, x = place()
    zr, za = z % 4, z // 4
    grp = y * 4 + zr
    bar = pltpu.get_barrier_semaphore()

    loads = [
        pltpu.make_async_copy(anc_h, anc, in_sem.at[0]),
        pltpu.make_async_copy(pat_h, pat, in_sem.at[1]),
        pltpu.make_async_copy(rhs_h, rhs, in_sem.at[2]),
        pltpu.make_async_copy(inv_h, inv, in_sem.at[3]),
        pltpu.make_async_copy(pan_h, pan.at[:, pl.ds(0, 4)], in_sem.at[4]),
        pltpu.make_async_copy(
            trhs_h.at[pl.ds(pl.multiple_of((grp // 2) * 128 + c * 64 + (grp % 2) * 32, 32), 32)], trhs, in_sem.at[5]
        ),
        pltpu.make_async_copy(tinv_h.at[0], tops.at[x], in_sem.at[6]),
    ]
    for load in loads:
        load.start()

    def signal(sem, to):
        pl.semaphore_signal(sem, inc=1, device_id=to, device_id_type=MESH)

    for dy in (2, 1, 3, 0):
        for d in (-2, 2, -1, 1, 0):
            if (dy, d) != (0, 0) and (d != 2 or dy == 0):
                signal(bar, device((y - dy) % 4, (z - d) % NZ, c, x))
    for k in (2, 1, 3):
        signal(bar, device(y, z, c, (x + k) % 4))
    signal(bar, device(y, z, 1 - c, x))
    if not CHAIN:
        for k in (2, 1, 3):
            signal(bar, device(y, (z + 4 * k) % NZ, c, x))

    pan[:, 4] = jnp.zeros((LV, 128, 128), BF)
    loads[0].wait()
    loads[1].wait()
    for l in range(LV):
        stored = [jnp.where(pat[k, l] != 0, k, 4) for k in range(4)]
        blocks = [anc[k, l] for k in range(4)]
        for b in range(NB):
            kk = 4
            for k in range(4):
                kk = jnp.where(blocks[k] == b, stored[k], kk)
            which[b, l] = kk
    loads[2].wait()
    loads[3].wait()
    for l in range(LV):
        rows = pl.ds(l * 128, 128)
        solved[rows] = jnp.dot(inv[l], rhs[rows], preferred_element_type=F32).astype(BF)
    outs = [
        pltpu.make_async_copy(solved, solved_o, out_sem.at[0]),
        pltpu.make_async_copy(flip, flip_o, out_sem.at[1]),
        pltpu.make_async_copy(invt, invt_o, out_sem.at[2]),
        pltpu.make_async_copy(mine_red, red_o.at[c, grp], out_sem.at[3]),
        pltpu.make_async_copy(tops, tops_o, out_sem.at[4]),
        pltpu.make_async_copy(topt, topt_o, out_sem.at[5]),
    ]
    loads[4].wait()

    def half(j, core):
        first = 2 * ((y + ORDER[j]) % 4)
        rows = pl.ds(pl.multiple_of(core * 64, 64), 64)
        left = jnp.concatenate(
            [
                jnp.concatenate([pan[l, which[first + e, l], rows] for l in range(LV)], axis=1)
                for e in range(2)
            ],
            axis=0,
        )
        return jnp.dot(left, solved[...], preferred_element_type=F32)

    for j in range(4):
        half_tx[j] = half(j, 1 - c).astype(BF)
        if j == 0:
            pl.semaphore_wait(bar, 20 if CHAIN else 23)
            if CHAIN:
                for k in (2, -2):
                    signal(near, device(y, (z + k) % NZ, c, x))
        send(half_tx.at[j], half_rx.at[j], half_s, half_r.at[j], device(y, z, 1 - c, x))
    for j in range(4):
        dy = ORDER[j]
        part = half(j, c)
        take(half_rx.at[j], half_r.at[j])
        tx1[j] = (part + half_rx[j].astype(F32)).astype(BF)
        for r in range(4):
            d = (r - z + 2) % 4
            slot = dy * 4 + d
            piece = tx1.at[j, pl.ds(r * 32, 32)]
            if dy:
                send(piece, rx1.at[slot], s1_s, s1_r, device((y + dy) % 4, (z + d - 2) % NZ, c, x))
            else:

                @pl.when(d != 2)
                def _():
                    send(piece, rx1.at[slot], s1_s, s1_r, device(y, (z + d - 2) % NZ, c, x))

                @pl.when(d == 2)
                def _():
                    rx1[2] = piece[...]

    if CHAIN:
        pl.semaphore_wait(near, 2)
        for k in (4, -4):
            signal(far, device(y, (z + k) % NZ, c, x))
    outs[0].start()
    loads[6].wait()
    if TSEND:
        for k in (2, 1, 3):
            send(tops.at[x], tops.at[x], t_s, t_r, device(y, z, c, (x + k) % 4))

    def turn(l, _):
        flip[l] = pan[l, 0:4].reshape(512, 128).T
        return 0

    def turn_inv(l, _):
        invt[l] = inv[l].T
        return 0

    lax.fori_loop(0, LV // 2, turn, 0)
    take(rx1.at[pl.ds(0, 15)], s1_r)
    total = rx1[0].astype(F32)
    for slot in range(1, 16):
        total = total + rx1[slot].astype(F32)
    tx2[...] = total.astype(BF)
    if CHAIN:
        pl.semaphore_wait(far, 2)
    for k in (2, 1, 3):
        send(tx2, rx2.at[za], s2_s, s2_r, device(y, (z + 4 * k) % NZ, c, x))
    rx2[za] = tx2[...]
    lax.fori_loop(LV // 2, LV, turn, 0)
    outs[1].start()
    lax.fori_loop(0, LV, turn_inv, 0)
    outs[2].start()
    if TSEND:
        take(tops.at[pl.ds(0, 3)], t_r)
    outs[4].start()
    for t in range(4):
        topt[t] = tops[t].T
    outs[5].start()
    loads[5].wait()
    take(rx2.at[pl.ds(0, 3)], s2_r)
    total = rx2[0].astype(F32)
    for k in range(1, 4):
        total = total + rx2[k].astype(F32)
    mine_red[...] = (trhs[...].astype(F32) - total).astype(BF)
    for dy in (2, 1, 3, 0):
        for d in (-2, 1, -1, 0):
            if (dy, d) != (0, 0):
                send(mine_red, red_o.at[c, grp], s3_s, s3_r.at[dy], device((y + dy) % 4, (z + d) % NZ, c, x))
    outs[3].start()
    outs[3].wait()
    for dy in (0, 1, 3, 2):
        from_y = (y - dy) % 4
        quarter = red_o.at[c, pl.ds(pl.multiple_of(from_y * 4, 4), 4)]
        take(red_o.at[c, pl.ds(0, 3 if dy == 0 else 4)], s3_r.at[dy])
        send(quarter, quarter, s4_s, s4_r.at[dy], device(y, z, 1 - c, x))
    take(half_tx, half_s)
    take(rx1.at[pl.ds(0, 15)], s1_s)
    take(rx2.at[pl.ds(0, 3)], s2_s)
    take(rx1.at[pl.ds(0, 15)], s3_s)
    if TSEND:
        take(tops.at[pl.ds(0, 3)], t_s)
    for k in (0, 1, 2, 4, 5):
        outs[k].wait()
    for dy in (0, 1, 3, 2):
        take(red_o.at[c, pl.ds(0, 4)], s4_r.at[dy])
    take(red_o.at[c], s4_s)


def backward_kernel(red, tops, topt, solved, flip, invt, anc_h, pat_h, out_h, x_h, known, rem, out, anc, pat, sems):
    loads = [
        pltpu.make_async_copy(anc_h, anc, sems.at[LV + 1]),
        pltpu.make_async_copy(pat_h, pat, sems.at[LV + 2]),
    ]
    for load in loads:
        load.start()
    known[pl.ds(NB, 1)] = jnp.zeros((1, 128, 128), BF)
    middles = []
    for t in range(4):
        parts = []
        for j in range(2):
            for core in range(2):
                for h in range(2):
                    parts.append(red[core, t * 4 + 2 * j + h])
        middles.append(jnp.dot(tops[t], jnp.concatenate(parts, axis=0), preferred_element_type=F32).astype(BF))
    for t in range(4):
        top = jnp.dot(topt[t], middles[t], preferred_element_type=F32).astype(BF)
        known[pl.ds(2 * t, 2)] = top.reshape(2, 128, 128)
    x_copy = pltpu.make_async_copy(known.at[pl.ds(0, NB)], x_h, sems.at[LV])
    x_copy.start()
    for load in loads:
        load.wait()
    for l in range(LV):
        parts = []
        for k in range(4):
            parts.append(known[jnp.where(pat[k, l] != 0, anc[k, l], NB)])
        back = jnp.dot(flip[l], jnp.concatenate(parts, axis=0), preferred_element_type=F32)
        rem[l] = (solved[l].astype(F32) - back).astype(BF)
    copies = []
    for l in range(LV):
        out[l] = jnp.dot(invt[l], rem[l], preferred_element_type=F32)
        if l % PER == PER - 1:
            some = pl.ds(l + 1 - PER, PER)
            copies.append(pltpu.make_async_copy(out.at[some], out_h.at[some], sems.at[l]))
            copies[-1].start()
    for copy in copies:
        copy.wait()
    x_copy.wait()


def shards(leaf_rhs, leaf_inverse, panels, ancestors, pattern, top_rhs, top_inverse):
    hbm = pl.BlockSpec(memory_space=pltpu.HBM)
    any_spec = pl.BlockSpec(memory_space=pl.ANY)
    vmem = pl.BlockSpec(memory_space=pltpu.VMEM)
    V, D = pltpu.VMEM, pltpu.SemaphoreType.DMA
    anc, pat = ancestors.T, pattern.T
    shape = jax.ShapeDtypeStruct
    solved, flip, invt, tops, topt, red = pl.pallas_call(
        forward_kernel,
        out_shape=(
            shape((2048, 128), BF), shape((LV, 128, 512), BF), shape((LV, 128, 128), BF),
            shape((4, 256, 256), BF), shape((4, 256, 256), BF), shape((2, 16, 32, 128), BF),
        ),
        in_specs=[hbm] * 7,
        out_specs=(any_spec,) * 6,
        scratch_shapes=[
            V((2048, 128), BF), V((LV, 128, 128), BF), V((LV, 5, 128, 128), BF),
            pltpu.SMEM((4, LV), jnp.int32), pltpu.SMEM((4, LV), jnp.int32), pltpu.SMEM((NB, LV), jnp.int32),
            V((2048, 128), BF), V((LV, 128, 512), BF), V((LV, 128, 128), BF), V((4, 256, 256), BF), V((4, 256, 256), BF),
            V((4, 128, 128), BF), V((4, 128, 128), BF), V((4, 128, 128), BF), V((16, 32, 128), BF),
            V((32, 128), BF), V((4, 32, 128), BF), V((32, 128), BF), V((32, 128), BF),
            D((7,)), D((6,)), pltpu.SemaphoreType.REGULAR, pltpu.SemaphoreType.REGULAR,
            D, D((4,)), D, D, D, D, D, D((4,)), D, D((4,)), D, D,
        ],
        compiler_params=pltpu.CompilerParams(collective_id=0, has_side_effects=True, vmem_limit_bytes=20 * 2**20),
        cost_estimate=pl.CostEstimate(flops=700_000_000, bytes_accessed=4_000_000, transcendentals=0),
        name="forward",
    )(*(pltpu.with_memory_space_constraint(a, pltpu.HBM) for a in (leaf_rhs, leaf_inverse, panels, anc, pat, top_rhs, top_inverse)))
    leaf_solution, top_solution = pl.pallas_call(
        backward_kernel,
        out_shape=(shape((LV, 128, 128), F32), shape((NB, 128, 128), BF)),
        in_specs=[vmem] * 6 + [any_spec] * 2,
        out_specs=(hbm, hbm),
        scratch_shapes=[
            V((NB + 1, 128, 128), BF), V((LV, 128, 128), BF), V((LV, 128, 128), F32),
            pltpu.SMEM((4, LV), jnp.int32), pltpu.SMEM((4, LV), jnp.int32), D((LV + 3,)),
        ],
        compiler_params=pltpu.CompilerParams(vmem_limit_bytes=20 * 2**20),
        cost_estimate=pl.CostEstimate(flops=400_000_000, bytes_accessed=4_000_000, transcendentals=0),
        name="backward",
    )(red, tops, topt, solved.reshape(LV, 128, 128), flip, invt, anc, pat)
    return leaf_solution.reshape(LV * 128, 128), top_solution.reshape(NB * 128, 128)


def solution(mesh):
    placed = (
        P("leaf", "rhs"),
        P("leaf", None, None),
        P("leaf", None, None, None),
        P("leaf", None),
        P("leaf", None),
        P(None, "rhs"),
        P("rhs", None, None),
    )
    return jax.shard_map(
        shards, mesh=mesh, in_specs=placed, out_specs=(P("leaf", "rhs"), P(None, "rhs")), check_vma=False
    )
```

```python
import functools
import jax
import jax.numpy as jnp
from jax import lax
from jax.experimental import pallas as pl
from jax.experimental.pallas import tpu as pltpu
from jax.sharding import PartitionSpec as P

MESH = pl.DeviceIdType.MESH
BF = jnp.bfloat16
F32 = jnp.float32
NY, NZ = 4, 16
LV = 16
NB = 8
TSEND = True
ORDER = (2, 1, 3, 0)
PER = 2
SPLIT = 4


def place():
    leaf = lax.axis_index("leaf")
    return leaf // (2 * NZ), (leaf // 2) % NZ, leaf % 2, lax.axis_index("rhs")


def device(y, z, c, x):
    return ((y * NZ + z) * 2 + c, x)


def send(src, dst, send_sem, recv_sem, to):
    pltpu.make_async_remote_copy(
        src_ref=src, dst_ref=dst, send_sem=send_sem, recv_sem=recv_sem, device_id=to, device_id_type=MESH
    ).start()


def take(like, sem):
    pltpu.make_async_copy(like, like, sem).wait()


def forward_kernel(
    rhs_h, inv_h, pan_h, anc_h, pat_h, trhs_h, tinv_h, solved_o, flip_o, invt_o, tops_o, topt_o, red_o,
    rhs, inv, pan, anc, pat, which, solved, flip, invt, tops, topt,
    tx1, rx1, tx2, rx2, trhs, mine_red,
    in_sem, out_sem, near, far, s1_s, s1_r, s2_s, s2_r, s3_s, s3_r, t_s, t_r,
):
    y, z, c, x = place()
    zr, za = z % 4, z // 4
    bar = pltpu.get_barrier_semaphore()

    loads = [
        pltpu.make_async_copy(anc_h, anc, in_sem.at[0]),
        pltpu.make_async_copy(pat_h, pat, in_sem.at[1]),
        pltpu.make_async_copy(rhs_h, rhs, in_sem.at[2]),
        pltpu.make_async_copy(inv_h, inv, in_sem.at[3]),
        pltpu.make_async_copy(trhs_h.at[pl.ds(pl.multiple_of((y * 8 + c * 4 + zr) * 32, 32), 32)], trhs, in_sem.at[4]),
        pltpu.make_async_copy(tinv_h.at[0], tops.at[x], in_sem.at[5]),
    ]
    pan_loads = []
    for k in range(SPLIT):
        some = pl.ds(k * (LV // SPLIT), LV // SPLIT)
        pan_loads.append(pltpu.make_async_copy(pan_h.at[some], pan.at[some, pl.ds(0, 4)], in_sem.at[6 + k]))
    loads = loads[:4] + pan_loads + loads[4:]
    for load in loads:
        load.start()

    def signal(sem, to):
        pl.semaphore_signal(sem, inc=1, device_id=to, device_id_type=MESH)

    for dy in (2, 1, 3):
        for d in range(4):
            for core in range(2):
                signal(bar, device((y - dy) % 4, (z - (c - 2) - d) % NZ, core, x))
    for d in range(4):
        signal(bar, device(y, (z - (c - 2) - d) % NZ, 1 - c, x))
    for d in (-2, 2, -1, 1):
        signal(bar, device(y, (z + d) % NZ, c, x))
    for k in (2, 1, 3):
        signal(bar, device(y, z, c, (x + k) % 4))

    pan[:, 4] = jnp.zeros((LV, 128, 128), BF)
    for load in loads[:4]:
        load.wait()
    for l in range(LV):
        stored = [jnp.where(pat[k, l] != 0, k, 4) for k in range(4)]
        blocks = [anc[k, l] for k in range(4)]
        for b in range(NB):
            kk = 4
            for k in range(4):
                kk = jnp.where(blocks[k] == b, stored[k], kk)
            which[b, l] = kk
        rows = pl.ds(l * 128, 128)
        solved[rows] = jnp.dot(inv[l], rhs[rows], preferred_element_type=F32).astype(BF)
    outs = [
        pltpu.make_async_copy(solved, solved_o, out_sem.at[0]),
        pltpu.make_async_copy(flip, flip_o, out_sem.at[1]),
        pltpu.make_async_copy(invt, invt_o, out_sem.at[2]),
        pltpu.make_async_copy(mine_red, red_o.at[y, c * 4 + zr], out_sem.at[3]),
        pltpu.make_async_copy(tops, tops_o, out_sem.at[4]),
        pltpu.make_async_copy(topt, topt_o, out_sem.at[5]),
    ]
    for load in pan_loads:
        load.wait()

    for j, dy in enumerate(ORDER):
        left = []
        for e in range(2):
            b = 2 * ((y + dy) % 4) + e
            left.append(jnp.concatenate([pan[l, which[b, l]] for l in range(LV)], axis=1))
        tx1[j] = jnp.dot(jnp.concatenate(left, axis=0), solved[...], preferred_element_type=F32).astype(BF)
        if j == 0:
            pl.semaphore_wait(bar, 35)
            for k in (2, -2):
                signal(near, device(y, (z + k) % NZ, c, x))
        for core in range(2):
            low = core - 2
            for r in range(4):
                d = (r - z - low) % 4
                slot = (dy * 4 + d) * 2 + c
                piece = tx1.at[j, pl.ds((core * 4 + r) * 32, 32)]
                if dy:
                    send(piece, rx1.at[slot], s1_s, s1_r, device((y + dy) % 4, (z + d + low) % NZ, core, x))
                else:
                    mine = (d + low == 0) & (c == core)

                    @pl.when(jnp.logical_not(mine))
                    def _():
                        send(piece, rx1.at[slot], s1_s, s1_r, device(y, (z + d + low) % NZ, core, x))

                    @pl.when(mine)
                    def _():
                        rx1[slot] = piece[...]

    pl.semaphore_wait(near, 2)
    for k in (4, -4):
        signal(far, device(y, (z + k) % NZ, c, x))
    outs[0].start()
    loads[-1].wait()
    if TSEND:
        for k in (2, 1, 3):
            send(tops.at[x], tops.at[x], t_s, t_r, device(y, z, c, (x + k) % 4))

    def turn(l, _):
        flip[l] = pan[l, 0:4].reshape(512, 128).T
        return 0

    def turn_inv(l, _):
        invt[l] = inv[l].T
        return 0

    lax.fori_loop(0, LV // 2, turn, 0)
    take(rx1.at[pl.ds(0, 31)], s1_r)
    total = rx1[0].astype(F32)
    for slot in range(1, 32):
        total = total + rx1[slot].astype(F32)
    tx2[...] = total.astype(BF)
    pl.semaphore_wait(far, 2)
    for k in (2, 1, 3):
        send(tx2, rx2.at[za], s2_s, s2_r, device(y, (z + 4 * k) % NZ, c, x))
    rx2[za] = tx2[...]
    lax.fori_loop(LV // 2, LV, turn, 0)
    outs[1].start()
    lax.fori_loop(0, LV, turn_inv, 0)
    outs[2].start()
    if TSEND:
        take(tops.at[pl.ds(0, 3)], t_r)
    outs[4].start()
    for t in range(4):
        topt[t] = tops[t].T
    outs[5].start()
    loads[-2].wait()
    take(rx2.at[pl.ds(0, 3)], s2_r)
    total = rx2[0].astype(F32)
    for k in range(1, 4):
        total = total + rx2[k].astype(F32)
    mine_red[...] = (trhs[...].astype(F32) - total).astype(BF)
    place_red = red_o.at[y, c * 4 + zr]
    for dy in (2, 1, 3):
        for core in range(2):
            for d in (0, 3, 1, 2):
                send(mine_red, place_red, s3_s, s3_r, device((y + dy) % 4, (z + core - 2 + d) % NZ, core, x))
    for d in range(4):
        send(mine_red, place_red, s3_s, s3_r, device(y, (z - 1 - c + d) % NZ, 1 - c, x))
    for d in (4 * c - 2, 1, -1):
        send(mine_red, place_red, s3_s, s3_r, device(y, (z + d) % NZ, c, x))
    outs[3].start()
    take(rx1.at[pl.ds(0, 31)], s1_s)
    take(rx2.at[pl.ds(0, 3)], s2_s)
    if TSEND:
        take(tops.at[pl.ds(0, 3)], t_s)
    for out in outs:
        out.wait()
    take(rx1.at[pl.ds(0, 31)], s3_r)
    take(rx1.at[pl.ds(0, 31)], s3_s)


def backward_kernel(red, tops, topt, solved, flip, invt, anc_h, pat_h, out_h, x_h, known, rem, out, anc, pat, sems):
    loads = [
        pltpu.make_async_copy(anc_h, anc, sems.at[LV + 1]),
        pltpu.make_async_copy(pat_h, pat, sems.at[LV + 2]),
    ]
    for load in loads:
        load.start()
    known[pl.ds(NB, 1)] = jnp.zeros((1, 128, 128), BF)
    middles = []
    for t in range(4):
        middles.append(jnp.dot(tops[t], red[t].reshape(256, 128), preferred_element_type=F32).astype(BF))
    for t in range(4):
        top = jnp.dot(topt[t], middles[t], preferred_element_type=F32).astype(BF)
        known[pl.ds(2 * t, 2)] = top.reshape(2, 128, 128)
    x_copy = pltpu.make_async_copy(known.at[pl.ds(0, NB)], x_h, sems.at[LV])
    x_copy.start()
    for load in loads:
        load.wait()
    for l in range(LV):
        parts = []
        for k in range(4):
            parts.append(known[jnp.where(pat[k, l] != 0, anc[k, l], NB)])
        back = jnp.dot(flip[l], jnp.concatenate(parts, axis=0), preferred_element_type=F32)
        rem[l] = (solved[l].astype(F32) - back).astype(BF)
    copies = []
    for l in range(LV):
        out[l] = jnp.dot(invt[l], rem[l], preferred_element_type=F32)
        if l % PER == PER - 1:
            some = pl.ds(l + 1 - PER, PER)
            copies.append(pltpu.make_async_copy(out.at[some], out_h.at[some], sems.at[l]))
            copies[-1].start()
    for copy in copies:
        copy.wait()
    x_copy.wait()


def shards(leaf_rhs, leaf_inverse, panels, ancestors, pattern, top_rhs, top_inverse):
    hbm = pl.BlockSpec(memory_space=pltpu.HBM)
    any_spec = pl.BlockSpec(memory_space=pl.ANY)
    vmem = pl.BlockSpec(memory_space=pltpu.VMEM)
    V, D = pltpu.VMEM, pltpu.SemaphoreType.DMA
    anc, pat = ancestors.T, pattern.T
    shape = jax.ShapeDtypeStruct
    solved, flip, invt, tops, topt, red = pl.pallas_call(
        forward_kernel,
        out_shape=(
            shape((2048, 128), BF), shape((LV, 128, 512), BF), shape((LV, 128, 128), BF),
            shape((4, 256, 256), BF), shape((4, 256, 256), BF), shape((4, 8, 32, 128), BF),
        ),
        in_specs=[hbm] * 7,
        out_specs=(any_spec,) * 6,
        scratch_shapes=[
            V((2048, 128), BF), V((LV, 128, 128), BF), V((LV, 5, 128, 128), BF),
            pltpu.SMEM((4, LV), jnp.int32), pltpu.SMEM((4, LV), jnp.int32), pltpu.SMEM((NB, LV), jnp.int32),
            V((2048, 128), BF), V((LV, 128, 512), BF), V((LV, 128, 128), BF), V((4, 256, 256), BF), V((4, 256, 256), BF),
            V((4, 256, 128), BF), V((32, 32, 128), BF),
            V((32, 128), BF), V((4, 32, 128), BF), V((32, 128), BF), V((32, 128), BF),
            D((6 + SPLIT,)), D((6,)), pltpu.SemaphoreType.REGULAR, pltpu.SemaphoreType.REGULAR,
            D, D, D, D, D, D, D, D,
        ],
        compiler_params=pltpu.CompilerParams(collective_id=0, has_side_effects=True, vmem_limit_bytes=20 * 2**20),
        cost_estimate=pl.CostEstimate(flops=700_000_000, bytes_accessed=4_000_000, transcendentals=0),
        name="forward",
    )(*(pltpu.with_memory_space_constraint(a, pltpu.HBM) for a in (leaf_rhs, leaf_inverse, panels, anc, pat, top_rhs, top_inverse)))
    leaf_solution, top_solution = pl.pallas_call(
        backward_kernel,
        out_shape=(shape((LV, 128, 128), F32), shape((NB, 128, 128), BF)),
        in_specs=[vmem] * 6 + [any_spec] * 2,
        out_specs=(hbm, hbm),
        scratch_shapes=[
            V((NB + 1, 128, 128), BF), V((LV, 128, 128), BF), V((LV, 128, 128), F32),
            pltpu.SMEM((4, LV), jnp.int32), pltpu.SMEM((4, LV), jnp.int32), D((LV + 3,)),
        ],
        compiler_params=pltpu.CompilerParams(vmem_limit_bytes=20 * 2**20),
        cost_estimate=pl.CostEstimate(flops=400_000_000, bytes_accessed=4_000_000, transcendentals=0),
        name="backward",
    )(red, tops, topt, solved.reshape(LV, 128, 128), flip, invt, anc, pat)
    return leaf_solution.reshape(LV * 128, 128), top_solution.reshape(NB * 128, 128)


def solution(mesh):
    placed = (
        P("leaf", "rhs"),
        P("leaf", None, None),
        P("leaf", None, None, None),
        P("leaf", None),
        P("leaf", None),
        P(None, "rhs"),
        P("rhs", None, None),
    )
    return jax.shard_map(
        shards, mesh=mesh, in_specs=placed, out_specs=(P("leaf", "rhs"), P(None, "rhs")), check_vma=False
    )
```

```python
import functools
import jax
import jax.numpy as jnp
from jax import lax
from jax.experimental import pallas as pl
from jax.experimental.pallas import tpu as pltpu
from jax.sharding import PartitionSpec as P

MESH = pl.DeviceIdType.MESH
BF = jnp.bfloat16
F32 = jnp.float32
NY, NZ = 4, 16
LV = 16
NB = 8
TSEND = True
ORDER = (2, 1, 3, 0)
PER = 2
SPLIT = 4


def place():
    leaf = lax.axis_index("leaf")
    return leaf // (2 * NZ), (leaf // 2) % NZ, leaf % 2, lax.axis_index("rhs")


def device(y, z, c, x):
    return ((y * NZ + z) * 2 + c, x)


def send(src, dst, send_sem, recv_sem, to):
    pltpu.make_async_remote_copy(
        src_ref=src, dst_ref=dst, send_sem=send_sem, recv_sem=recv_sem, device_id=to, device_id_type=MESH
    ).start()


def take(like, sem):
    pltpu.make_async_copy(like, like, sem).wait()


def forward_kernel(
    rhs_h, inv_h, pan_h, anc_h, pat_h, trhs_h, tinv_h, solved_o, flip_o, invt_o, tops_o, topt_o, red_o,
    rhs, inv, pan, anc, pat, which, solved, flip, invt, tops, topt,
    tx1, rx1, tx2, rx2, trhs, mine_red,
    in_sem, out_sem, near, far, s1_s, s1_r, s2_s, s2_r, s3_s, s3_r, t_s, t_r,
):
    y, z, c, x = place()
    za = z // 4
    zc = (z + 2) % 4
    bar = pltpu.get_barrier_semaphore()

    loads = [
        pltpu.make_async_copy(anc_h, anc, in_sem.at[0]),
        pltpu.make_async_copy(pat_h, pat, in_sem.at[1]),
        pltpu.make_async_copy(rhs_h, rhs, in_sem.at[2]),
        pltpu.make_async_copy(inv_h, inv, in_sem.at[3]),
        pltpu.make_async_copy(trhs_h.at[pl.ds(pl.multiple_of((y * 8 + c * 4 + zc) * 32, 32), 32)], trhs, in_sem.at[4]),
        pltpu.make_async_copy(tinv_h.at[0], tops.at[x], in_sem.at[5]),
    ]
    pan_loads = []
    for k in range(SPLIT):
        some = pl.ds(k * (LV // SPLIT), LV // SPLIT)
        pan_loads.append(pltpu.make_async_copy(pan_h.at[some], pan.at[some, pl.ds(0, 4)], in_sem.at[6 + k]))
    loads = loads[:4] + pan_loads + loads[4:]
    for load in loads:
        load.start()

    def signal(sem, to):
        pl.semaphore_signal(sem, inc=1, device_id=to, device_id_type=MESH)

    for dy in (2, 1, 3):
        for d in range(4):
            for core in range(2):
                signal(bar, device((y - dy) % 4, (z - (c - 2) - d) % NZ, core, x))
    for d in range(4):
        signal(bar, device(y, (z - (c - 2) - d) % NZ, 1 - c, x))
    for d in (-2, 2, -1, 1):
        signal(bar, device(y, (z + d) % NZ, c, x))
    for k in (2, 1, 3):
        signal(bar, device(y, z, c, (x + k) % 4))

    pan[:, 4] = jnp.zeros((LV, 128, 128), BF)
    for load in loads[:4]:
        load.wait()
    for l in range(LV):
        stored = [jnp.where(pat[k, l] != 0, k, 4) for k in range(4)]
        blocks = [anc[k, l] for k in range(4)]
        for b in range(NB):
            kk = 4
            for k in range(4):
                kk = jnp.where(blocks[k] == b, stored[k], kk)
            which[b, l] = kk
        rows = pl.ds(l * 128, 128)
        solved[rows] = jnp.dot(inv[l], rhs[rows], preferred_element_type=F32).astype(BF)
    outs = [
        pltpu.make_async_copy(solved, solved_o, out_sem.at[0]),
        pltpu.make_async_copy(flip, flip_o, out_sem.at[1]),
        pltpu.make_async_copy(invt, invt_o, out_sem.at[2]),
        pltpu.make_async_copy(mine_red, red_o.at[y, c * 4 + zc], out_sem.at[3]),
        pltpu.make_async_copy(tops, tops_o, out_sem.at[4]),
        pltpu.make_async_copy(topt, topt_o, out_sem.at[5]),
    ]
    for load in pan_loads:
        load.wait()

    for j, dy in enumerate(ORDER):
        left = []
        for e in range(2):
            b = 2 * ((y + dy) % 4) + e
            left.append(jnp.concatenate([pan[l, which[b, l]] for l in range(LV)], axis=1))
        tx1[j] = jnp.dot(jnp.concatenate(left, axis=0), solved[...], preferred_element_type=F32).astype(BF)
        if j == 0:
            pl.semaphore_wait(bar, 35)
            for k in (2, -2):
                signal(near, device(y, (z + k) % NZ, c, x))
        for core in range(2):
            low = core - 2
            for r in range(4):
                d = (r - z - low) % 4
                slot = (dy * 4 + d) * 2 + c
                piece = tx1.at[j, pl.ds((core * 4 + r) * 32, 32)]
                if dy:
                    send(piece, rx1.at[slot], s1_s, s1_r, device((y + dy) % 4, (z + d + low) % NZ, core, x))
                else:
                    mine = (d + low == 0) & (c == core)

                    @pl.when(jnp.logical_not(mine))
                    def _():
                        send(piece, rx1.at[slot], s1_s, s1_r, device(y, (z + d + low) % NZ, core, x))

                    @pl.when(mine)
                    def _():
                        rx1[slot] = piece[...]

    pl.semaphore_wait(near, 2)
    for k in (4, -4):
        signal(far, device(y, (z + k) % NZ, c, x))
    outs[0].start()
    loads[-1].wait()
    if TSEND:
        for k in (2, 1, 3):
            send(tops.at[x], tops.at[x], t_s, t_r, device(y, z, c, (x + k) % 4))

    def turn(l, _):
        flip[l] = pan[l, 0:4].reshape(512, 128).T
        return 0

    def turn_inv(l, _):
        invt[l] = inv[l].T
        return 0

    lax.fori_loop(0, LV // 2, turn, 0)
    take(rx1.at[pl.ds(0, 31)], s1_r)
    total = rx1[0].astype(F32)
    for slot in range(1, 32):
        total = total + rx1[slot].astype(F32)
    tx2[...] = total.astype(BF)
    pl.semaphore_wait(far, 2)
    for k in (6, -6, 2, -2):
        send(tx2, rx2.at[za], s2_s, s2_r, device(y, (z + k) % NZ, c, x))
    lax.fori_loop(LV // 2, LV, turn, 0)
    outs[1].start()
    lax.fori_loop(0, LV, turn_inv, 0)
    outs[2].start()
    if TSEND:
        take(tops.at[pl.ds(0, 3)], t_r)
    outs[4].start()
    for t in range(4):
        topt[t] = tops[t].T
    outs[5].start()
    loads[-2].wait()
    take(rx2, s2_r)
    total = rx2[0].astype(F32)
    for k in range(1, 4):
        total = total + rx2[k].astype(F32)
    mine_red[...] = (trhs[...].astype(F32) - total).astype(BF)
    place_red = red_o.at[y, c * 4 + zc]
    for dy in (2, 1, 3):
        for core in range(2):
            for d in (0, 3, 1, 2):
                send(mine_red, place_red, s3_s, s3_r, device((y + dy) % 4, (z + core - 2 + d) % NZ, core, x))
    for d in range(4):
        send(mine_red, place_red, s3_s, s3_r, device(y, (z - 1 - c + d) % NZ, 1 - c, x))
    for d in (4 * c - 2, 1, -1):
        send(mine_red, place_red, s3_s, s3_r, device(y, (z + d) % NZ, c, x))
    outs[3].start()
    take(rx1.at[pl.ds(0, 31)], s1_s)
    take(rx2, s2_s)
    if TSEND:
        take(tops.at[pl.ds(0, 3)], t_s)
    for out in outs:
        out.wait()
    take(rx1.at[pl.ds(0, 31)], s3_r)
    take(rx1.at[pl.ds(0, 31)], s3_s)


def backward_kernel(red, tops, topt, solved, flip, invt, anc_h, pat_h, out_h, x_h, known, rem, out, anc, pat, sems):
    loads = [
        pltpu.make_async_copy(anc_h, anc, sems.at[LV + 1]),
        pltpu.make_async_copy(pat_h, pat, sems.at[LV + 2]),
    ]
    for load in loads:
        load.start()
    known[pl.ds(NB, 1)] = jnp.zeros((1, 128, 128), BF)
    middles = []
    for t in range(4):
        middles.append(jnp.dot(tops[t], red[t].reshape(256, 128), preferred_element_type=F32).astype(BF))
    for t in range(4):
        top = jnp.dot(topt[t], middles[t], preferred_element_type=F32).astype(BF)
        known[pl.ds(2 * t, 2)] = top.reshape(2, 128, 128)
    x_copy = pltpu.make_async_copy(known.at[pl.ds(0, NB)], x_h, sems.at[LV])
    x_copy.start()
    for load in loads:
        load.wait()
    for l in range(LV):
        parts = []
        for k in range(4):
            parts.append(known[jnp.where(pat[k, l] != 0, anc[k, l], NB)])
        back = jnp.dot(flip[l], jnp.concatenate(parts, axis=0), preferred_element_type=F32)
        rem[l] = (solved[l].astype(F32) - back).astype(BF)
    copies = []
    for l in range(LV):
        out[l] = jnp.dot(invt[l], rem[l], preferred_element_type=F32)
        if l % PER == PER - 1:
            some = pl.ds(l + 1 - PER, PER)
            copies.append(pltpu.make_async_copy(out.at[some], out_h.at[some], sems.at[l]))
            copies[-1].start()
    for copy in copies:
        copy.wait()
    x_copy.wait()


def shards(leaf_rhs, leaf_inverse, panels, ancestors, pattern, top_rhs, top_inverse):
    hbm = pl.BlockSpec(memory_space=pltpu.HBM)
    any_spec = pl.BlockSpec(memory_space=pl.ANY)
    vmem = pl.BlockSpec(memory_space=pltpu.VMEM)
    V, D = pltpu.VMEM, pltpu.SemaphoreType.DMA
    anc, pat = ancestors.T, pattern.T
    shape = jax.ShapeDtypeStruct
    solved, flip, invt, tops, topt, red = pl.pallas_call(
        forward_kernel,
        out_shape=(
            shape((2048, 128), BF), shape((LV, 128, 512), BF), shape((LV, 128, 128), BF),
            shape((4, 256, 256), BF), shape((4, 256, 256), BF), shape((4, 8, 32, 128), BF),
        ),
        in_specs=[hbm] * 7,
        out_specs=(any_spec,) * 6,
        scratch_shapes=[
            V((2048, 128), BF), V((LV, 128, 128), BF), V((LV, 5, 128, 128), BF),
            pltpu.SMEM((4, LV), jnp.int32), pltpu.SMEM((4, LV), jnp.int32), pltpu.SMEM((NB, LV), jnp.int32),
            V((2048, 128), BF), V((LV, 128, 512), BF), V((LV, 128, 128), BF), V((4, 256, 256), BF), V((4, 256, 256), BF),
            V((4, 256, 128), BF), V((32, 32, 128), BF),
            V((32, 128), BF), V((4, 32, 128), BF), V((32, 128), BF), V((32, 128), BF),
            D((6 + SPLIT,)), D((6,)), pltpu.SemaphoreType.REGULAR, pltpu.SemaphoreType.REGULAR,
            D, D, D, D, D, D, D, D,
        ],
        compiler_params=pltpu.CompilerParams(collective_id=0, has_side_effects=True, vmem_limit_bytes=20 * 2**20),
        cost_estimate=pl.CostEstimate(flops=700_000_000, bytes_accessed=4_000_000, transcendentals=0),
        name="forward",
    )(*(pltpu.with_memory_space_constraint(a, pltpu.HBM) for a in (leaf_rhs, leaf_inverse, panels, anc, pat, top_rhs, top_inverse)))
    leaf_solution, top_solution = pl.pallas_call(
        backward_kernel,
        out_shape=(shape((LV, 128, 128), F32), shape((NB, 128, 128), BF)),
        in_specs=[vmem] * 6 + [any_spec] * 2,
        out_specs=(hbm, hbm),
        scratch_shapes=[
            V((NB + 1, 128, 128), BF), V((LV, 128, 128), BF), V((LV, 128, 128), F32),
            pltpu.SMEM((4, LV), jnp.int32), pltpu.SMEM((4, LV), jnp.int32), D((LV + 3,)),
        ],
        compiler_params=pltpu.CompilerParams(vmem_limit_bytes=20 * 2**20),
        cost_estimate=pl.CostEstimate(flops=400_000_000, bytes_accessed=4_000_000, transcendentals=0),
        name="backward",
    )(red, tops, topt, solved.reshape(LV, 128, 128), flip, invt, anc, pat)
    return leaf_solution.reshape(LV * 128, 128), top_solution.reshape(NB * 128, 128)


def solution(mesh):
    placed = (
        P("leaf", "rhs"),
        P("leaf", None, None),
        P("leaf", None, None, None),
        P("leaf", None),
        P("leaf", None),
        P(None, "rhs"),
        P("rhs", None, None),
    )
    return jax.shard_map(
        shards, mesh=mesh, in_specs=placed, out_specs=(P("leaf", "rhs"), P(None, "rhs")), check_vma=False
    )
```

```python
import functools
import jax
import jax.numpy as jnp
from jax import lax
from jax.experimental import pallas as pl
from jax.experimental.pallas import tpu as pltpu
from jax.sharding import PartitionSpec as P

MESH = pl.DeviceIdType.MESH
BF = jnp.bfloat16
F32 = jnp.float32
NY, NZ = 4, 16
LV = 16
NB = 8
TSEND = True
ORDER = (2, 1, 3, 0)
PER = 2
SPLIT = 4


def place():
    leaf = lax.axis_index("leaf")
    return leaf // (2 * NZ), (leaf // 2) % NZ, leaf % 2, lax.axis_index("rhs")


def device(y, z, c, x):
    return ((y * NZ + z) * 2 + c, x)


def send(src, dst, send_sem, recv_sem, to):
    pltpu.make_async_remote_copy(
        src_ref=src, dst_ref=dst, send_sem=send_sem, recv_sem=recv_sem, device_id=to, device_id_type=MESH
    ).start()


def take(like, sem):
    pltpu.make_async_copy(like, like, sem).wait()


def forward_kernel(
    rhs_h, inv_h, pan_h, anc_h, pat_h, trhs_h, tinv_h, solved_o, flip_o, invt_o, tops_o, topt_o, red_o,
    rhs, inv, pan, anc, pat, which, solved, flip, invt, tops, topt,
    tx1, rx1, tx2, rx2, trhs, mine_red,
    in_sem, out_sem, near, far, s1_s, s1_r, s2_s, s2_r, s3_s, s3_r, t_s, t_r,
):
    y, z, c, x = place()
    za = z // 4
    zc = (z + 2) % 4
    bar = pltpu.get_barrier_semaphore()

    loads = [
        pltpu.make_async_copy(anc_h, anc, in_sem.at[0]),
        pltpu.make_async_copy(pat_h, pat, in_sem.at[1]),
        pltpu.make_async_copy(rhs_h, rhs, in_sem.at[2]),
        pltpu.make_async_copy(inv_h, inv, in_sem.at[3]),
        pltpu.make_async_copy(trhs_h.at[pl.ds(pl.multiple_of((y * 8 + c * 4 + zc) * 32, 32), 32)], trhs, in_sem.at[4]),
        pltpu.make_async_copy(tinv_h.at[0], tops.at[x], in_sem.at[5]),
    ]
    pan_loads = []
    for k in range(SPLIT):
        some = pl.ds(k * (LV // SPLIT), LV // SPLIT)
        pan_loads.append(pltpu.make_async_copy(pan_h.at[some], pan.at[some, pl.ds(0, 4)], in_sem.at[6 + k]))
    loads = loads[:4] + pan_loads + loads[4:]
    for load in loads:
        load.start()

    def signal(sem, to):
        pl.semaphore_signal(sem, inc=1, device_id=to, device_id_type=MESH)

    for dy in (2, 1, 3):
        for d in range(4):
            for core in range(2):
                signal(bar, device((y - dy) % 4, (z - (c - 2) - d) % NZ, core, x))
    for d in range(4):
        signal(bar, device(y, (z - (c - 2) - d) % NZ, 1 - c, x))
    for d in (-2, 2, -1, 1):
        signal(bar, device(y, (z + d) % NZ, c, x))
    for k in (2, 1, 3):
        signal(bar, device(y, z, c, (x + k) % 4))

    pan[:, 4] = jnp.zeros((LV, 128, 128), BF)
    for load in loads[:4]:
        load.wait()
    for l in range(LV):
        stored = [jnp.where(pat[k, l] != 0, k, 4) for k in range(4)]
        blocks = [anc[k, l] for k in range(4)]
        for b in range(NB):
            kk = 4
            for k in range(4):
                kk = jnp.where(blocks[k] == b, stored[k], kk)
            which[b, l] = kk
        rows = pl.ds(l * 128, 128)
        solved[rows] = jnp.dot(inv[l], rhs[rows], preferred_element_type=F32).astype(BF)
    outs = [
        pltpu.make_async_copy(solved, solved_o, out_sem.at[0]),
        pltpu.make_async_copy(flip, flip_o, out_sem.at[1]),
        pltpu.make_async_copy(invt, invt_o, out_sem.at[2]),
        pltpu.make_async_copy(mine_red, red_o.at[y, c * 4 + zc], out_sem.at[3]),
        pltpu.make_async_copy(tops, tops_o, out_sem.at[4]),
        pltpu.make_async_copy(topt, topt_o, out_sem.at[5]),
    ]
    for load in pan_loads:
        load.wait()

    for j, dy in enumerate(ORDER):
        left = []
        for e in range(2):
            b = 2 * ((y + dy) % 4) + e
            left.append(jnp.concatenate([pan[l, which[b, l]] for l in range(LV)], axis=1))
        tx1[j] = jnp.dot(jnp.concatenate(left, axis=0), solved[...], preferred_element_type=F32).astype(BF)
        if j == 0:
            pl.semaphore_wait(bar, 35)
            for k in (2, -2):
                signal(near, device(y, (z + k) % NZ, c, x))
        for d in range(4):
            for core in range(2):
                low = core - 2
                r = (z + low + d) % 4
                slot = (dy * 4 + d) * 2 + c
                piece = tx1.at[j, pl.ds(pl.multiple_of((core * 4 + r) * 32, 32), 32)]
                to = device((y + dy) % 4, (z + d + low) % NZ, core, x)
                if dy or d + low:
                    send(piece, rx1.at[slot], s1_s, s1_r, to)
                else:

                    @pl.when(c != core)
                    def _():
                        send(piece, rx1.at[slot], s1_s, s1_r, to)

                    @pl.when(c == core)
                    def _():
                        rx1[slot] = piece[...]

    pl.semaphore_wait(near, 2)
    for k in (4, -4):
        signal(far, device(y, (z + k) % NZ, c, x))
    outs[0].start()
    loads[-1].wait()
    if TSEND:
        for k in (2, 1, 3):
            send(tops.at[x], tops.at[x], t_s, t_r, device(y, z, c, (x + k) % 4))

    def turn(l, _):
        flip[l] = pan[l, 0:4].reshape(512, 128).T
        return 0

    def turn_inv(l, _):
        invt[l] = inv[l].T
        return 0

    lax.fori_loop(0, LV // 2, turn, 0)
    take(rx1.at[pl.ds(0, 31)], s1_r)
    total = rx1[0].astype(F32)
    for slot in range(1, 32):
        total = total + rx1[slot].astype(F32)
    tx2[...] = total.astype(BF)
    pl.semaphore_wait(far, 2)
    for k in (6, -6, 2, -2):
        send(tx2, rx2.at[za], s2_s, s2_r, device(y, (z + k) % NZ, c, x))
    lax.fori_loop(LV // 2, LV, turn, 0)
    outs[1].start()
    lax.fori_loop(0, LV, turn_inv, 0)
    outs[2].start()
    if TSEND:
        take(tops.at[pl.ds(0, 3)], t_r)
    outs[4].start()
    for t in range(4):
        topt[t] = tops[t].T
    outs[5].start()
    loads[-2].wait()
    take(rx2, s2_r)
    total = rx2[0].astype(F32)
    for k in range(1, 4):
        total = total + rx2[k].astype(F32)
    mine_red[...] = (trhs[...].astype(F32) - total).astype(BF)
    place_red = red_o.at[y, c * 4 + zc]
    for i in range(4):
        for up in range(4):
            dy = (up - y) % 4
            for core in range(2):
                base = (z + core - 2) % NZ
                d = (i + jnp.where(base > NZ - 4, NZ - base, 0)) % 4
                to = device((y + dy) % 4, (base + d) % NZ, core, x)
                @pl.when((dy != 0) | (core != c) | (d + core != 2))
                def _():
                    send(mine_red, place_red, s3_s, s3_r, to)

    outs[3].start()
    take(rx1.at[pl.ds(0, 31)], s1_s)
    take(rx2, s2_s)
    if TSEND:
        take(tops.at[pl.ds(0, 3)], t_s)
    for out in outs:
        out.wait()
    take(rx1.at[pl.ds(0, 31)], s3_r)
    take(rx1.at[pl.ds(0, 31)], s3_s)


def backward_kernel(red, tops, topt, solved, flip, invt, anc_h, pat_h, out_h, x_h, known, rem, out, anc, pat, sems):
    loads = [
        pltpu.make_async_copy(anc_h, anc, sems.at[LV + 1]),
        pltpu.make_async_copy(pat_h, pat, sems.at[LV + 2]),
    ]
    for load in loads:
        load.start()
    known[pl.ds(NB, 1)] = jnp.zeros((1, 128, 128), BF)
    middles = []
    for t in range(4):
        middles.append(jnp.dot(tops[t], red[t].reshape(256, 128), preferred_element_type=F32).astype(BF))
    for t in range(4):
        top = jnp.dot(topt[t], middles[t], preferred_element_type=F32).astype(BF)
        known[pl.ds(2 * t, 2)] = top.reshape(2, 128, 128)
    x_copy = pltpu.make_async_copy(known.at[pl.ds(0, NB)], x_h, sems.at[LV])
    x_copy.start()
    for load in loads:
        load.wait()
    for l in range(LV):
        parts = []
        for k in range(4):
            parts.append(known[jnp.where(pat[k, l] != 0, anc[k, l], NB)])
        back = jnp.dot(flip[l], jnp.concatenate(parts, axis=0), preferred_element_type=F32)
        rem[l] = (solved[l].astype(F32) - back).astype(BF)
    copies = []
    for l in range(LV):
        out[l] = jnp.dot(invt[l], rem[l], preferred_element_type=F32)
        if l % PER == PER - 1:
            some = pl.ds(l + 1 - PER, PER)
            copies.append(pltpu.make_async_copy(out.at[some], out_h.at[some], sems.at[l]))
            copies[-1].start()
    for copy in copies:
        copy.wait()
    x_copy.wait()


def shards(leaf_rhs, leaf_inverse, panels, ancestors, pattern, top_rhs, top_inverse):
    hbm = pl.BlockSpec(memory_space=pltpu.HBM)
    any_spec = pl.BlockSpec(memory_space=pl.ANY)
    vmem = pl.BlockSpec(memory_space=pltpu.VMEM)
    V, D = pltpu.VMEM, pltpu.SemaphoreType.DMA
    anc, pat = ancestors.T, pattern.T
    shape = jax.ShapeDtypeStruct
    solved, flip, invt, tops, topt, red = pl.pallas_call(
        forward_kernel,
        out_shape=(
            shape((2048, 128), BF), shape((LV, 128, 512), BF), shape((LV, 128, 128), BF),
            shape((4, 256, 256), BF), shape((4, 256, 256), BF), shape((4, 8, 32, 128), BF),
        ),
        in_specs=[hbm] * 7,
        out_specs=(any_spec,) * 6,
        scratch_shapes=[
            V((2048, 128), BF), V((LV, 128, 128), BF), V((LV, 5, 128, 128), BF),
            pltpu.SMEM((4, LV), jnp.int32), pltpu.SMEM((4, LV), jnp.int32), pltpu.SMEM((NB, LV), jnp.int32),
            V((2048, 128), BF), V((LV, 128, 512), BF), V((LV, 128, 128), BF), V((4, 256, 256), BF), V((4, 256, 256), BF),
            V((4, 256, 128), BF), V((32, 32, 128), BF),
            V((32, 128), BF), V((4, 32, 128), BF), V((32, 128), BF), V((32, 128), BF),
            D((6 + SPLIT,)), D((6,)), pltpu.SemaphoreType.REGULAR, pltpu.SemaphoreType.REGULAR,
            D, D, D, D, D, D, D, D,
        ],
        compiler_params=pltpu.CompilerParams(collective_id=0, has_side_effects=True, vmem_limit_bytes=20 * 2**20),
        cost_estimate=pl.CostEstimate(flops=700_000_000, bytes_accessed=4_000_000, transcendentals=0),
        name="forward",
    )(*(pltpu.with_memory_space_constraint(a, pltpu.HBM) for a in (leaf_rhs, leaf_inverse, panels, anc, pat, top_rhs, top_inverse)))
    leaf_solution, top_solution = pl.pallas_call(
        backward_kernel,
        out_shape=(shape((LV, 128, 128), F32), shape((NB, 128, 128), BF)),
        in_specs=[vmem] * 6 + [any_spec] * 2,
        out_specs=(hbm, hbm),
        scratch_shapes=[
            V((NB + 1, 128, 128), BF), V((LV, 128, 128), BF), V((LV, 128, 128), F32),
            pltpu.SMEM((4, LV), jnp.int32), pltpu.SMEM((4, LV), jnp.int32), D((LV + 3,)),
        ],
        compiler_params=pltpu.CompilerParams(vmem_limit_bytes=20 * 2**20),
        cost_estimate=pl.CostEstimate(flops=400_000_000, bytes_accessed=4_000_000, transcendentals=0),
        name="backward",
    )(red, tops, topt, solved.reshape(LV, 128, 128), flip, invt, anc, pat)
    return leaf_solution.reshape(LV * 128, 128), top_solution.reshape(NB * 128, 128)


def solution(mesh):
    placed = (
        P("leaf", "rhs"),
        P("leaf", None, None),
        P("leaf", None, None, None),
        P("leaf", None),
        P("leaf", None),
        P(None, "rhs"),
        P("rhs", None, None),
    )
    return jax.shard_map(
        shards, mesh=mesh, in_specs=placed, out_specs=(P("leaf", "rhs"), P(None, "rhs")), check_vma=False
    )
```

```python
import functools
import jax
import jax.numpy as jnp
from jax import lax
from jax.experimental import pallas as pl
from jax.experimental.pallas import tpu as pltpu
from jax.sharding import PartitionSpec as P

MESH = pl.DeviceIdType.MESH
BF = jnp.bfloat16
F32 = jnp.float32
NY, NZ = 4, 16
LV = 16
NB = 8
TSEND = True
ORDER = (2, 1, 3, 0)
PER = 2
AHEAD = 1
SPLIT = 4


def place():
    leaf = lax.axis_index("leaf")
    return leaf // (2 * NZ), (leaf // 2) % NZ, leaf % 2, lax.axis_index("rhs")


def device(y, z, c, x):
    return ((y * NZ + z) * 2 + c, x)


def send(src, dst, send_sem, recv_sem, to):
    pltpu.make_async_remote_copy(
        src_ref=src, dst_ref=dst, send_sem=send_sem, recv_sem=recv_sem, device_id=to, device_id_type=MESH
    ).start()


def take(like, sem):
    pltpu.make_async_copy(like, like, sem).wait()


def forward_kernel(
    rhs_h, inv_h, pan_h, anc_h, pat_h, trhs_h, tinv_h, solved_o, flip_o, invt_o, tops_o, topt_o, red_o,
    rhs, inv, pan, anc, pat, which, solved, flip, invt, tops, topt,
    tx1, rx1, tx2, rx2, trhs, mine_red,
    in_sem, out_sem, near, far, s1_s, s1_r, s2_s, s2_r, s3_s, s3_r, t_s, t_r,
):
    y, z, c, x = place()
    za = z // 4
    zc = (z + 2) % 4
    bar = pltpu.get_barrier_semaphore()

    loads = [
        pltpu.make_async_copy(anc_h, anc, in_sem.at[0]),
        pltpu.make_async_copy(pat_h, pat, in_sem.at[1]),
        pltpu.make_async_copy(rhs_h, rhs, in_sem.at[2]),
        pltpu.make_async_copy(inv_h, inv, in_sem.at[3]),
        pltpu.make_async_copy(trhs_h.at[pl.ds(pl.multiple_of((y * 8 + c * 4 + zc) * 32, 32), 32)], trhs, in_sem.at[4]),
        pltpu.make_async_copy(tinv_h.at[0], tops.at[x], in_sem.at[5]),
    ]
    pan_loads = []
    for k in range(SPLIT):
        some = pl.ds(k * (LV // SPLIT), LV // SPLIT)
        pan_loads.append(pltpu.make_async_copy(pan_h.at[some], pan.at[some, pl.ds(0, 4)], in_sem.at[6 + k]))
    loads = loads[:4] + pan_loads + loads[4:]
    for load in loads:
        load.start()

    def signal(sem, to):
        pl.semaphore_signal(sem, inc=1, device_id=to, device_id_type=MESH)

    for dy in (2, 1, 3):
        for d in range(4):
            for core in range(2):
                signal(bar, device((y - dy) % 4, (z - (c - 2) - d) % NZ, core, x))
    for d in range(4):
        signal(bar, device(y, (z - (c - 2) - d) % NZ, 1 - c, x))
    for d in (-2, 2, -1, 1):
        signal(bar, device(y, (z + d) % NZ, c, x))
    for k in (2, 1, 3):
        signal(bar, device(y, z, c, (x + k) % 4))

    pan[:, 4] = jnp.zeros((LV, 128, 128), BF)
    for load in loads[:4]:
        load.wait()
    for l in range(LV):
        stored = [jnp.where(pat[k, l] != 0, k, 4) for k in range(4)]
        blocks = [anc[k, l] for k in range(4)]
        for b in range(NB):
            kk = 4
            for k in range(4):
                kk = jnp.where(blocks[k] == b, stored[k], kk)
            which[b, l] = kk
        rows = pl.ds(l * 128, 128)
        solved[rows] = jnp.dot(inv[l], rhs[rows], preferred_element_type=F32).astype(BF)
    outs = [
        pltpu.make_async_copy(solved, solved_o, out_sem.at[0]),
        pltpu.make_async_copy(flip, flip_o, out_sem.at[1]),
        pltpu.make_async_copy(invt, invt_o, out_sem.at[2]),
        pltpu.make_async_copy(mine_red, red_o.at[y, c * 4 + zc], out_sem.at[3]),
        pltpu.make_async_copy(tops, tops_o, out_sem.at[4]),
        pltpu.make_async_copy(topt, topt_o, out_sem.at[5]),
    ]
    for load in pan_loads:
        load.wait()

    def multiply(j, dy):
        left = []
        for e in range(2):
            b = 2 * ((y + dy) % 4) + e
            left.append(jnp.concatenate([pan[l, which[b, l]] for l in range(LV)], axis=1))
        tx1[j] = jnp.dot(jnp.concatenate(left, axis=0), solved[...], preferred_element_type=F32).astype(BF)

    def spread(j, dy):
        for d in range(4):
            for core in range(2):
                low = core - 2
                r = (z + low + d) % 4
                slot = (dy * 4 + d) * 2 + c
                piece = tx1.at[j, pl.ds(pl.multiple_of((core * 4 + r) * 32, 32), 32)]
                to = device((y + dy) % 4, (z + d + low) % NZ, core, x)
                if dy or d + low:
                    send(piece, rx1.at[slot], s1_s, s1_r, to)
                else:

                    @pl.when(c != core)
                    def _():
                        send(piece, rx1.at[slot], s1_s, s1_r, to)

                    @pl.when(c == core)
                    def _():
                        rx1[slot] = piece[...]

    for j, dy in enumerate(ORDER):
        multiply(j, dy)
        if j == AHEAD:
            pl.semaphore_wait(bar, 35)
            for k in (2, -2):
                signal(near, device(y, (z + k) % NZ, c, x))
            for e in range(AHEAD):
                spread(e, ORDER[e])
        if j >= AHEAD:
            spread(j, dy)

    pl.semaphore_wait(near, 2)
    for k in (2, -2):
        signal(far, device(y, (z + k) % NZ, c, x))
    outs[0].start()
    loads[-1].wait()
    if TSEND:
        for k in (2, 1, 3):
            send(tops.at[x], tops.at[x], t_s, t_r, device(y, z, c, (x + k) % 4))

    def turn(l, _):
        flip[l] = pan[l, 0:4].reshape(512, 128).T
        return 0

    def turn_inv(l, _):
        invt[l] = inv[l].T
        return 0

    lax.fori_loop(0, LV // 2, turn, 0)
    take(rx1.at[pl.ds(0, 31)], s1_r)
    total = rx1[0].astype(F32)
    for slot in range(1, 32):
        total = total + rx1[slot].astype(F32)
    tx2[...] = total.astype(BF)
    pl.semaphore_wait(far, 2)
    for k in (6, -6, 2, -2):
        send(tx2, rx2.at[za], s2_s, s2_r, device(y, (z + k) % NZ, c, x))
    lax.fori_loop(LV // 2, LV, turn, 0)
    outs[1].start()
    lax.fori_loop(0, LV, turn_inv, 0)
    outs[2].start()
    if TSEND:
        take(tops.at[pl.ds(0, 3)], t_r)
    outs[4].start()
    for t in range(4):
        topt[t] = tops[t].T
    outs[5].start()
    loads[-2].wait()
    take(rx2, s2_r)
    total = rx2[0].astype(F32)
    for k in range(1, 4):
        total = total + rx2[k].astype(F32)
    mine_red[...] = (trhs[...].astype(F32) - total).astype(BF)
    place_red = red_o.at[y, c * 4 + zc]
    for i in range(4):
        for up in range(4):
            dy = (up - y) % 4
            for core in (1, 0):
                base = (z + core - 2) % NZ
                d = (i + jnp.where(base > NZ - 4, NZ - base, 0)) % 4
                to = device((y + dy) % 4, (base + d) % NZ, core, x)
                @pl.when((dy != 0) | (core != c) | (d + core != 2))
                def _():
                    send(mine_red, place_red, s3_s, s3_r, to)

    outs[3].start()
    take(rx1.at[pl.ds(0, 31)], s1_s)
    take(rx2, s2_s)
    if TSEND:
        take(tops.at[pl.ds(0, 3)], t_s)
    for out in outs:
        out.wait()
    take(rx1.at[pl.ds(0, 31)], s3_r)
    take(rx1.at[pl.ds(0, 31)], s3_s)


def backward_kernel(red, tops, topt, solved, flip, invt, anc_h, pat_h, out_h, x_h, known, rem, out, anc, pat, sems):
    loads = [
        pltpu.make_async_copy(anc_h, anc, sems.at[LV + 1]),
        pltpu.make_async_copy(pat_h, pat, sems.at[LV + 2]),
    ]
    for load in loads:
        load.start()
    known[pl.ds(NB, 1)] = jnp.zeros((1, 128, 128), BF)
    middles = []
    for t in range(4):
        middles.append(jnp.dot(tops[t], red[t].reshape(256, 128), preferred_element_type=F32).astype(BF))
    for t in range(4):
        top = jnp.dot(topt[t], middles[t], preferred_element_type=F32).astype(BF)
        known[pl.ds(2 * t, 2)] = top.reshape(2, 128, 128)
    x_copy = pltpu.make_async_copy(known.at[pl.ds(0, NB)], x_h, sems.at[LV])
    x_copy.start()
    for load in loads:
        load.wait()
    for l in range(LV):
        parts = []
        for k in range(4):
            parts.append(known[jnp.where(pat[k, l] != 0, anc[k, l], NB)])
        back = jnp.dot(flip[l], jnp.concatenate(parts, axis=0), preferred_element_type=F32)
        rem[l] = (solved[l].astype(F32) - back).astype(BF)
    copies = []
    for l in range(LV):
        out[l] = jnp.dot(invt[l], rem[l], preferred_element_type=F32)
        if l % PER == PER - 1:
            some = pl.ds(l + 1 - PER, PER)
            copies.append(pltpu.make_async_copy(out.at[some], out_h.at[some], sems.at[l]))
            copies[-1].start()
    for copy in copies:
        copy.wait()
    x_copy.wait()


def shards(leaf_rhs, leaf_inverse, panels, ancestors, pattern, top_rhs, top_inverse):
    hbm = pl.BlockSpec(memory_space=pltpu.HBM)
    any_spec = pl.BlockSpec(memory_space=pl.ANY)
    vmem = pl.BlockSpec(memory_space=pltpu.VMEM)
    V, D = pltpu.VMEM, pltpu.SemaphoreType.DMA
    anc, pat = ancestors.T, pattern.T
    shape = jax.ShapeDtypeStruct
    solved, flip, invt, tops, topt, red = pl.pallas_call(
        forward_kernel,
        out_shape=(
            shape((2048, 128), BF), shape((LV, 128, 512), BF), shape((LV, 128, 128), BF),
            shape((4, 256, 256), BF), shape((4, 256, 256), BF), shape((4, 8, 32, 128), BF),
        ),
        in_specs=[hbm] * 7,
        out_specs=(any_spec,) * 6,
        scratch_shapes=[
            V((2048, 128), BF), V((LV, 128, 128), BF), V((LV, 5, 128, 128), BF),
            pltpu.SMEM((4, LV), jnp.int32), pltpu.SMEM((4, LV), jnp.int32), pltpu.SMEM((NB, LV), jnp.int32),
            V((2048, 128), BF), V((LV, 128, 512), BF), V((LV, 128, 128), BF), V((4, 256, 256), BF), V((4, 256, 256), BF),
            V((4, 256, 128), BF), V((32, 32, 128), BF),
            V((32, 128), BF), V((4, 32, 128), BF), V((32, 128), BF), V((32, 128), BF),
            D((6 + SPLIT,)), D((6,)), pltpu.SemaphoreType.REGULAR, pltpu.SemaphoreType.REGULAR,
            D, D, D, D, D, D, D, D,
        ],
        compiler_params=pltpu.CompilerParams(collective_id=0, has_side_effects=True, vmem_limit_bytes=20 * 2**20),
        cost_estimate=pl.CostEstimate(flops=700_000_000, bytes_accessed=4_000_000, transcendentals=0),
        name="forward",
    )(*(pltpu.with_memory_space_constraint(a, pltpu.HBM) for a in (leaf_rhs, leaf_inverse, panels, anc, pat, top_rhs, top_inverse)))
    leaf_solution, top_solution = pl.pallas_call(
        backward_kernel,
        out_shape=(shape((LV, 128, 128), F32), shape((NB, 128, 128), BF)),
        in_specs=[vmem] * 6 + [any_spec] * 2,
        out_specs=(hbm, hbm),
        scratch_shapes=[
            V((NB + 1, 128, 128), BF), V((LV, 128, 128), BF), V((LV, 128, 128), F32),
            pltpu.SMEM((4, LV), jnp.int32), pltpu.SMEM((4, LV), jnp.int32), D((LV + 3,)),
        ],
        compiler_params=pltpu.CompilerParams(vmem_limit_bytes=20 * 2**20),
        cost_estimate=pl.CostEstimate(flops=400_000_000, bytes_accessed=4_000_000, transcendentals=0),
        name="backward",
    )(red, tops, topt, solved.reshape(LV, 128, 128), flip, invt, anc, pat)
    return leaf_solution.reshape(LV * 128, 128), top_solution.reshape(NB * 128, 128)


def solution(mesh):
    placed = (
        P("leaf", "rhs"),
        P("leaf", None, None),
        P("leaf", None, None, None),
        P("leaf", None),
        P("leaf", None),
        P(None, "rhs"),
        P("rhs", None, None),
    )
    return jax.shard_map(
        shards, mesh=mesh, in_specs=placed, out_specs=(P("leaf", "rhs"), P(None, "rhs")), check_vma=False
    )
```
